256 devices in a mesh: gx: 8 (over z), gy: 4 (over y_hi, core), gz: 8 (over x, y_lo).
Axes of the slice: x: 4, y: 4 (y_hi: 2, y_lo: 2; y = y_hi * 2 + y_lo), z: 8, core: 2. Of those that a mesh axis runs over, the one named last changes fastest.
Arguments:
- tokens: bfloat16 [1536, 8192], P(('gx', 'gy'), 'gz'), may hold values from -6 to 6
- cotangent: bfloat16 [1536, 8192], P(('gx', 'gy'), 'gz'), may hold values from -6 to 6
- gate_weight: bfloat16 [8192, 14336], P('gz', ('gx', 'gy')), may hold values from -0.0625 to 0.0625
- up_weight: bfloat16 [8192, 14336], P('gz', ('gx', 'gy')), may hold values from -0.0625 to 0.0625
- down_weight: bfloat16 [14336, 8192], P(('gx', 'gy'), 'gz'), may hold values from -0.046875 to 0.046875
Outputs:
- input_grad: bfloat16 [1536, 8192], P(('gx', 'gy'), 'gz')
- gate_grad: bfloat16 [8192, 14336], P('gz', ('gx', 'gy'))
- up_grad: bfloat16 [8192, 14336], P('gz', ('gx', 'gy'))
- down_grad: bfloat16 [14336, 8192], P(('gx', 'gy'), 'gz')
The draws below stay inside these ranges and needn't reach their ends.
All inputs are finite; a program needn't handle non-finite values.
Results may differ from the reference program's by a relative error of at most 0.0055.
Values may be sent and summed in bfloat16 or wider, within the bound.
A program may use at most 128 MiB of HBM per device.

```python
import jax
import jax.numpy as jnp
from jax import lax

D = 8192
FF = 14336
TOKENS = 1536


def shard_levels(own_key, shape, pieces, smallest, largest):
    loudness, own = 1.0, jax.random.fold_in(own_key, 6)
    for position, parts in pieces:
        steps = jnp.exp(jax.random.uniform(jax.random.fold_in(own, position), (parts,), jnp.float32, smallest / len(pieces), largest / len(pieces)))
        loudness = loudness * jnp.repeat(steps, shape[position] // parts).reshape([-1 if axis == position else 1 for axis in range(len(shape))])
    return loudness


def noise(own_key, dims, spread, most, split=(), dtype=jnp.bfloat16):
    factor_of = shard_levels(own_key, dims, split, -0.22, 0.18) if split else 1.0
    drawn = jax.random.normal(own_key, dims, jnp.float32) * spread * factor_of
    return jnp.minimum(jnp.maximum(drawn, -most), most).astype(dtype)


def setup_inputs(seed: int = 0) -> dict:
    splits = jax.random.split(jax.random.key(seed), 6)
    tokens = noise(splits[0], (TOKENS, D), 1.0, 6.0, ((0, 32), (1, 8)))
    cotangent = noise(splits[1], (TOKENS, D), 1.0, 6.0, ((0, 32), (1, 8)))
    gate_weight = noise(splits[2], (D, FF), D ** -0.5, 0.0625, ((0, 8), (1, 32)))
    up_weight = noise(splits[3], (D, FF), D ** -0.5, 0.0625, ((0, 8), (1, 32)))
    down_weight = noise(splits[4], (FF, D), FF ** -0.5, 0.046875, ((0, 32), (1, 8)))
    return {"tokens": tokens, "cotangent": cotangent, "gate_weight": gate_weight, "up_weight": up_weight, "down_weight": down_weight}


def outer_sum(left, right):
    return lax.dot_general(left, right, (((0,), (0,)), ((), ())), preferred_element_type=jnp.float32)


def reference(tokens, cotangent, gate_weight, up_weight, down_weight):
    gate = jnp.dot(tokens, gate_weight, preferred_element_type=jnp.float32)
    up = jnp.dot(tokens, up_weight, preferred_element_type=jnp.float32)
    sigmoid_gate = jax.nn.sigmoid(gate)
    hidden = (gate * sigmoid_gate * up).astype(jnp.bfloat16)
    hidden_grad = lax.dot_general(cotangent, down_weight, (((1,), (1,)), ((), ())), preferred_element_type=jnp.float32)
    up_part = (hidden_grad * gate * sigmoid_gate).astype(jnp.bfloat16)
    gate_part = (hidden_grad * up * sigmoid_gate * (1.0 + gate * (1.0 - sigmoid_gate))).astype(jnp.bfloat16)
    back_gate = lax.dot_general(gate_part, gate_weight, (((1,), (1,)), ((), ())), preferred_element_type=jnp.float32)
    back_up = lax.dot_general(up_part, up_weight, (((1,), (1,)), ((), ())), preferred_element_type=jnp.float32)
    input_grad = (back_gate + back_up).astype(jnp.bfloat16)
    gate_grad = outer_sum(tokens, gate_part).astype(jnp.bfloat16)
    up_grad = outer_sum(tokens, up_part).astype(jnp.bfloat16)
    down_grad = outer_sum(hidden, cotangent).astype(jnp.bfloat16)
    return input_grad, gate_grad, up_grad, down_grad
```

```python
import jax
import jax.numpy as jnp
from jax import lax
from jax.sharding import PartitionSpec as P

BLOCKS = ("gx", "gy")


def contract(left, right, dims):
    return lax.dot_general(left, right, ((dims[:1], dims[1:]), ((), ())), preferred_element_type=jnp.float32)


def summed(terms, axes, parts):
    rows, columns = terms.shape
    sent = terms.astype(jnp.bfloat16).reshape(parts, rows // parts, columns)
    landed = lax.all_to_all(sent, axes, split_axis=0, concat_axis=0)
    return jnp.sum(landed.astype(jnp.float32), axis=0)


def solution(mesh):
    depth = mesh.shape["gz"]
    blocks = mesh.shape["gx"] * mesh.shape["gy"]

    def on_device(tokens, cotangent, gate_weight, up_weight, down_weight):
        tokens_all = lax.all_gather(tokens, BLOCKS, axis=0, tiled=True)
        cotangent_all = lax.all_gather(cotangent, BLOCKS, axis=0, tiled=True)
        hidden_units = gate_weight.shape[1]
        terms = jnp.concatenate(
            [
                contract(tokens_all, gate_weight, (1, 0)).astype(jnp.bfloat16),
                contract(tokens_all, up_weight, (1, 0)).astype(jnp.bfloat16),
                contract(cotangent_all, down_weight, (1, 1)).astype(jnp.bfloat16),
            ],
            axis=1,
        )
        sums = summed(terms, "gz", depth)
        gate, up, hidden_grad = jnp.split(sums, [hidden_units, 2 * hidden_units], axis=1)
        sigmoid_gate = jax.nn.sigmoid(gate)
        hidden = gate * sigmoid_gate * up
        up_part = hidden_grad * gate * sigmoid_gate
        gate_part = hidden_grad * up * sigmoid_gate * (1.0 + gate * (1.0 - sigmoid_gate))
        parts = jnp.concatenate([hidden, up_part, gate_part], axis=1).astype(jnp.bfloat16)
        parts = lax.all_gather(parts, "gz", axis=0, tiled=True)
        hidden, up_part, gate_part = jnp.split(parts, [hidden_units, 2 * hidden_units], axis=1)
        input_term = contract(gate_part, gate_weight, (1, 1)) + contract(up_part, up_weight, (1, 1))
        input_grad = summed(input_term, BLOCKS, blocks).astype(jnp.bfloat16)
        gate_grad = contract(tokens_all, gate_part, (0, 0)).astype(jnp.bfloat16)
        up_grad = contract(tokens_all, up_part, (0, 0)).astype(jnp.bfloat16)
        down_grad = contract(hidden, cotangent_all, (0, 0)).astype(jnp.bfloat16)
        return input_grad, gate_grad, up_grad, down_grad

    by_row, by_column = P(BLOCKS, "gz"), P("gz", BLOCKS)
    return jax.shard_map(
        on_device,
        mesh=mesh,
        in_specs=(by_row, by_row, by_column, by_column, by_row),
        out_specs=(by_row, by_column, by_column, by_row),
        check_vma=False,
    )
```

```python
import functools

import jax
import jax.numpy as jnp
from jax import lax
from jax.experimental import pallas as pl
from jax.experimental.pallas import tpu as pltpu
from jax.sharding import PartitionSpec as P

F32, BF16 = jnp.float32, jnp.bfloat16
SLOTS = (0, 1, -1, 2, -2, 3, -3, 4)
CHUNKS = (128, 384, 384, 384, 256)
OFFSETS = tuple(sum(CHUNKS[:i]) for i in range(len(CHUNKS)))
COPIES = 224


def dot_nn(a, b):
    return lax.dot_general(a, b, (((1,), (0,)), ((), ())), preferred_element_type=F32)


def dot_nt(a, b):
    return lax.dot_general(a, b, (((1,), (1,)), ((), ())), preferred_element_type=F32)


def dot_tn(a, b):
    return lax.dot_general(a, b, (((0,), (0,)), ((), ())), preferred_element_type=F32)


def kernel(
    tok_in, cot_in, gw_in, uw_in, dw_in,
    ig_out, gg_out, ug_out, dg_out,
    act, gw, uw, wgu, dw,
    gu_s1, gu_r1, gu_own, gu_s2, gu_r2,
    h_s1, h_own, h_r1, h_s2, h_r2, h_fin,
    pa, pb, ip, d_r1, d_s2, d_r2, d_s3, d_r3,
    acc_gu, acc_d, gg_v, ug_v, dg_v, ig_v,
    send_sem, recv_sem, local_sem,
):
    rows, units = tok_in.shape[0], gw_in.shape[1]
    z, gy, gz = lax.axis_index("gx"), lax.axis_index("gy"), lax.axis_index("gz")
    yh, core, x, yl = gy // 2, gy % 2, gz // 2, gz % 2
    sibling = (z, yh * 2 + (1 - core), gz)
    far = (z, (1 - yh) * 2 + core, gz)
    near = (z, gy, x * 2 + (1 - yl))

    def along_z(d):
        return (lax.rem(z + 8 + d, 8), gy, gz)

    def x_of(d):
        return lax.rem(x + d, 4)

    def along_x(d):
        return (z, gy, x_of(d) * 2 + yl)

    def at(start, n):
        return pl.ds(pl.multiple_of(start, 16), n)

    copies = []

    def send(src, dst, device):
        i = len(copies)
        copy = pltpu.make_async_remote_copy(
            src_ref=src, dst_ref=dst, send_sem=send_sem.at[i], recv_sem=recv_sem.at[i],
            device_id=device, device_id_type=pl.DeviceIdType.MESH,
        )
        copy.start()
        copies.append(copy)
        return copy

    locals_ = []

    def local(src, dst):
        copy = pltpu.make_async_copy(src, dst, local_sem.at[len(locals_)])
        copy.start()
        locals_.append(copy)
        return copy

    own = [local(tok_in, act.at[0, pl.ds(0, rows)]), local(cot_in, act.at[1, pl.ds(0, rows)])]
    weights = [local(gw_in, gw), local(uw_in, uw), local(dw_in, dw)]

    barrier = pltpu.get_barrier_semaphore()
    peers = [sibling, far, near] + [along_x(d) for d in (1, 2, 3)] + [along_z(d) for d in range(1, 8)]
    for peer in peers:
        pl.semaphore_signal(barrier, inc=1, device_id=peer, device_id_type=pl.DeviceIdType.MESH)
    pl.semaphore_wait(barrier, len(peers))

    got, sib = {}, {}
    slot = {d: s * 4 * rows for s, d in enumerate(SLOTS)}

    def part(d, h, which=None):
        span = pl.ds(slot[d] + h * rows, rows)
        return act.at[:, span] if which is None else act.at[which, span]

    def ring(j, h):
        for sign in (1, -1):
            which = None if j < 4 else (0 if sign == 1 else 1)
            src, dst = -sign * (j - 1), (-sign * j if j < 4 else 4)
            got[sign, j, h] = send(part(src, h, which), part(dst, h, which), along_z(sign))

    def to_sibling(d, which=None):
        a, b = pl.ds(slot[d], 2 * rows), pl.ds(slot[d] + 2 * rows, 2 * rows)
        if which is None:
            return send(act.at[:, a], act.at[:, b], sibling)
        return send(act.at[which, a], act.at[which, b], sibling)

    def start_a():
        for copy in own:
            copy.wait()
        yh_copy = send(part(0, 0), part(0, 1), far)
        ring(1, 0)
        first = send(act.at[:, pl.ds(0, rows)], act.at[:, pl.ds(2 * rows, rows)], sibling)
        yh_copy.wait_recv()
        ring(1, 1)
        second = send(act.at[:, pl.ds(rows, rows)], act.at[:, pl.ds(3 * rows, rows)], sibling)
        for copy in weights:
            copy.wait()
        wgu[...] = jnp.concatenate([gw[...], uw[...]], axis=1)
        first.wait_recv()
        second.wait_recv()

    def forward(j, h):
        for sign in (1, -1):
            got[sign, j, h].wait_recv()
        if j < 4:
            ring(j + 1, h)
        if h == 1:
            if j < 4:
                sib[j] = [to_sibling(j), to_sibling(-j)]
            else:
                sib[j] = [to_sibling(4, 0), to_sibling(4, 1)]

    def siblings(j):
        for copy in sib[j]:
            copy.wait_recv()

    gu1, gu2, h1, h2 = {}, {}, {}, {}

    def s1(k):
        o, n = OFFSETS[k], CHUNKS[k]
        q, r = n // 2, n // 8
        half = pl.ds(o // 2, q)
        gu_s1[half] = dot_nn(act[0, at(o + (1 - yl) * q, q)], wgu[...]).astype(BF16)
        gu1[k] = send(gu_s1.at[half], gu_r1.at[half], near)
        term = dot_nt(act[1, pl.ds(o, n)], dw[...])
        h_own[pl.ds(o, n)] = term
        h_s1[pl.ds(o, n)] = term.astype(BF16)
        h1[k] = [
            send(h_s1.at[at(o + y * q + x_of(d) * r, r)], h_r1.at[d - 1, y, pl.ds(o // 8, r)], along_x(d))
            for d in (1, 3, 2) for y in (0, 1)
        ]
        gu_own[half] = dot_nn(act[0, at(o + yl * q, q)], wgu[...])

    def s2(k):
        o, n = OFFSETS[k], CHUNKS[k]
        q, r = n // 2, n // 8
        half, piece = pl.ds(o // 2, q), pl.ds(o // 8, r)
        gu1[k].wait_recv()
        gu_s2[half] = (gu_own[half] + gu_r1[half].astype(F32)).astype(BF16)
        gu2[k] = [
            send(gu_s2.at[at(o // 2 + x_of(d) * r, r)], gu_r2.at[d - 1, piece], along_x(d)) for d in (1, 3, 2)
        ]
        for copy in h1[k]:
            copy.wait_recv()

        def total(y):
            value = h_own[at(o + y * q + x * r, r)]
            for d in range(3):
                value = value + h_r1[d, y, piece].astype(F32)
            return value

        h_s2[piece] = total(1 - yl).astype(BF16)
        h2[k] = send(h_s2.at[piece], h_r2.at[piece], near)
        h_fin[piece] = total(yl)

    pa_y, pa_x, pb_y, pb_x, pa_xx, pb_yy = {}, {}, {}, {}, {}, {}

    def s3(k):
        o, n = OFFSETS[k], CHUNKS[k]
        q, r = n // 2, n // 8
        piece, mine = pl.ds(o // 8, r), at(o + yl * q + x * r, r)
        for copy in gu2[k]:
            copy.wait_recv()
        h2[k].wait_recv()
        kept = at(o // 2 + x * r, r)
        gu = gu_own[kept] + gu_r1[kept].astype(F32)
        for d in range(3):
            gu = gu + gu_r2[d, piece].astype(F32)
        hidden_grad = h_fin[piece] + h_r2[piece].astype(F32)
        gate, up = gu[:, :units], gu[:, units:]
        sigmoid_gate = jax.nn.sigmoid(gate)
        pb[mine] = (gate * sigmoid_gate * up).astype(BF16)
        up_part = hidden_grad * gate * sigmoid_gate
        gate_part = hidden_grad * up * sigmoid_gate * (1.0 + gate * (1.0 - sigmoid_gate))
        pa[mine] = jnp.concatenate([gate_part, up_part], axis=1).astype(BF16)
        pa_y[k] = send(pa.at[mine], pa.at[mine], near)
        pb_x[k] = [send(pb.at[mine], pb.at[mine], along_x(d)) for d in (1, 3, 2)]
        pa_x[k] = [send(pa.at[mine], pa.at[mine], along_x(d)) for d in (1, 3, 2)]
        pb_y[k] = send(pb.at[mine], pb.at[mine], near)

    def s4(k):
        o, n = OFFSETS[k], CHUNKS[k]
        q, r = n // 2, n // 8
        pa_y[k].wait_recv()
        other = at(o + (1 - yl) * q + x * r, r)
        pa_xx[k] = [send(pa.at[other], pa.at[other], along_x(d)) for d in (1, 3, 2)]
        pb_yy[k] = []
        for copy, d in zip(pb_x[k], (1, 3, 2)):
            copy.wait_recv()
            theirs = at(o + yl * q + x_of(4 - d) * r, r)
            pb_yy[k].append(send(pb.at[theirs], pb.at[theirs], near))

    def s5(k):
        for copy in pa_x[k] + pa_xx[k]:
            copy.wait_recv()
        span = pl.ds(OFFSETS[k], CHUNKS[k])
        ip[span] = dot_nt(pa[span], wgu[...])

    def s6(k):
        span = pl.ds(OFFSETS[k], CHUNKS[k])
        pb_y[k].wait_recv()
        for copy in pb_yy[k]:
            copy.wait_recv()
        gu_term = dot_tn(act[0, span], pa[span])
        acc_gu[...] = gu_term if k == 0 else acc_gu[...] + gu_term
        d_term = dot_tn(pb[span], act[1, span])
        acc_d[...] = d_term if k == 0 else acc_d[...] + d_term

    dc, dy, dz = {}, {}, {}

    def d1(s):
        dc[s] = send(ip.at[pl.ds((s * 4 + 2) * rows, 2 * rows)], d_r1.at[s], sibling)

    def d2(s):
        dc[s].wait_recv()
        d_s2[s] = (ip[pl.ds((s * 4 + 1) * rows, rows)] + d_r1[s, pl.ds(rows, rows)]).astype(BF16)
        dy[s] = send(d_s2.at[s], d_r2.at[s], far)

    def d3(s):
        dy[s].wait_recv()
        value = ip[pl.ds(s * 4 * rows, rows)] + d_r1[s, pl.ds(0, rows)] + d_r2[s].astype(F32)
        if s == 0:
            ip[pl.ds(0, rows)] = value
        else:
            d_s3[s] = value.astype(BF16)
            dz[s] = send(d_s3.at[s], d_r3.at[s - 1], along_z(SLOTS[s]))

    def d4():
        value = ip[pl.ds(0, rows)]
        for s in range(1, 8):
            dz[s].wait_recv()
            value = value + d_r3[s - 1].astype(F32)
        ig_v[...] = value.astype(BF16)

    start_a()
    s1(0)
    forward(1, 0)
    forward(1, 1)
    siblings(1)
    s1(1)
    s2(0)
    forward(2, 0)
    s3(0)
    forward(2, 1)
    siblings(2)
    s1(2)
    s2(1)
    s4(0)
    forward(3, 0)
    forward(3, 1)
    siblings(3)
    s1(3)
    s3(1)
    s5(0)
    forward(4, 0)
    forward(4, 1)
    s6(0)
    siblings(4)
    s1(4)
    s2(2)
    s4(1)
    s3(2)
    s5(1)
    d1(0)
    d1(1)
    s6(1)
    s2(3)
    s4(2)
    s3(3)
    d2(1)
    d2(0)
    s5(2)
    d1(2)
    d1(3)
    s2(4)
    s6(2)
    d3(1)
    d3(0)
    s4(3)
    s3(4)
    d2(2)
    d2(3)
    s5(3)
    d1(4)
    d1(5)
    s4(4)
    d3(2)
    d3(3)
    s6(3)
    d2(4)
    d2(5)
    s5(4)
    d1(7)
    d1(6)
    d3(4)
    d3(5)
    d2(7)
    d2(6)
    s6(4)
    d3(7)
    d3(6)
    gg_v[...] = acc_gu[:, :units].astype(BF16)
    ug_v[...] = acc_gu[:, units:].astype(BF16)
    dg_v[...] = acc_d[...].astype(BF16)
    outs = [local(gg_v, gg_out), local(ug_v, ug_out), local(dg_v, dg_out)]
    d4()
    outs.append(local(ig_v, ig_out))
    for copy in copies:
        copy.wait_send()
    for copy in outs:
        copy.wait()


def on_device(tokens, cotangent, gate_weight, up_weight, down_weight):
    rows, width = tokens.shape
    units = gate_weight.shape[1]
    n = rows * 32
    scratch = [
        ((2, n, width), BF16), ((width, units), BF16), ((width, units), BF16),
        ((width, 2 * units), BF16), ((units, width), BF16),
        ((n // 2, 2 * units), BF16), ((n // 2, 2 * units), BF16), ((n // 2, 2 * units), F32),
        ((n // 2, 2 * units), BF16), ((3, n // 8, 2 * units), BF16),
        ((n, units), BF16), ((n, units), F32), ((3, 2, n // 8, units), BF16),
        ((n // 8, units), BF16), ((n // 8, units), BF16), ((n // 8, units), F32),
        ((n, 2 * units), BF16), ((n, units), BF16),
        ((n, width), F32), ((8, 2 * rows, width), F32), ((8, rows, width), BF16),
        ((8, rows, width), BF16), ((8, rows, width), BF16), ((7, rows, width), BF16),
        ((width, 2 * units), F32), ((units, width), F32),
        ((width, units), BF16), ((width, units), BF16), ((units, width), BF16), ((rows, width), BF16),
    ]
    flops = 16 * n * width * units
    return pl.pallas_call(
        kernel,
        out_shape=[
            jax.ShapeDtypeStruct(a.shape, BF16) for a in (tokens, gate_weight, up_weight, down_weight)
        ],
        in_specs=[pl.BlockSpec(memory_space=pl.ANY)] * 5,
        out_specs=[pl.BlockSpec(memory_space=pl.ANY)] * 4,
        scratch_shapes=[pltpu.VMEM(shape, dtype) for shape, dtype in scratch]
        + [
            pltpu.SemaphoreType.DMA((COPIES,)),
            pltpu.SemaphoreType.DMA((COPIES,)),
            pltpu.SemaphoreType.DMA((16,)),
        ],
        compiler_params=pltpu.CompilerParams(
            collective_id=0, has_side_effects=True, vmem_limit_bytes=60 * 2**20
        ),
        cost_estimate=pl.CostEstimate(flops=flops, bytes_accessed=6 * 2**20, transcendentals=n * units // 8),
    )(tokens, cotangent, gate_weight, up_weight, down_weight)


def solution(mesh):
    blocks = ("gx", "gy")
    by_row, by_column = P(blocks, "gz"), P("gz", blocks)
    return jax.shard_map(
        on_device,
        mesh=mesh,
        in_specs=(by_row, by_row, by_column, by_column, by_row),
        out_specs=(by_row, by_column, by_column, by_row),
        check_vma=False,
    )
```

```python
import jax
import jax.numpy as jnp
from jax import lax
from jax.experimental import pallas as pl
from jax.experimental.pallas import tpu as pltpu
from jax.sharding import PartitionSpec as P

F32, BF16 = jnp.float32, jnp.bfloat16
SLOTS = (0, 1, -1, 2, -2, 3, -3, 4)
UNITS = ((0, 0), (0, 1), (1, 0), (-1, 0), (1, 1), (-1, 1), (2, 0), (-2, 0), (2, 1), (-2, 1), (3, 0), (-3, 0), (3, 1), (-3, 1), (4, 0), (4, 1))
CHUNKS = (128, 128, 128, 128, 128, 128, 128, 128, 128, 128, 128, 128)
X_FIRST = (True, False, False, False, False, True, False, True, False, True, False, False)
FORWARD = (True, False, True, True, True, True, True, True, True, True, True, True)
GROUPS = ((0, 1), (2, 3), (4, 5), (6, 7), (8, 9), (10, 11))
NEAR_Z = (1, -1, 2, -2)
ORDER = (
    ("A0",), ("R", 1, 0), ("A1",), ("s1a", 2), ("s1a", 0), ("s1a", 1), ("s1b", 0), ("s1b", 1), ("s1b", 2),
    ("s2a", 0), ("s2b", 1), ("s2a", 2), ("s2b", 2), ("R", 2, 0), ("s2b", 0), ("s2a", 1), ("R", 1, 1),
    ("s1a", 5), ("s1b", 5), ("s1a", 3), ("s1a", 4), ("s1b", 3), ("s1b", 4), ("s3", 0), ("s3b", 0), ("s3", 2),
    ("s3b", 2), ("s3", 1), ("s3b", 1), ("s2a", 5), ("R", 3, 0), ("s2b", 3), ("s4a", 0), ("R", 2, 1), ("s2b", 4),
    ("s4b", 0), ("s2b", 5), ("s4b", 2), ("s4a", 2), ("s1a", 6), ("s1a", 7), ("s4f1", 0), ("s1b", 6), ("s1b", 7),
    ("s4f1", 2), ("s2a", 3), ("s2a", 4), ("s4a", 1), ("s4b", 1), ("s4c", 0), ("s4f2", 0), ("s4c", 2),
    ("R", 4, 0), ("s3", 5), ("s3b", 5), ("s4f2", 2), ("R", 3, 1), ("s1a", 9), ("s2a", 7), ("s1a", 10),
    ("s2b", 6), ("s1b", 9), ("s1b", 10), ("s4a", 5), ("s2a", 6), ("s1a", 8), ("s1b", 8), ("s2b", 7),
    ("R", 4, 1), ("s3", 3), ("s4b", 5), ("s3b", 3), ("s3", 4), ("s3b", 4), ("s1a", 11), ("s1b", 11), ("s5", 0),
    ("d1", 0, 0), ("s5", 1), ("d1", 0, 1), ("s6", 0), ("s4f1", 5), ("s2a", 9), ("s5", 2), ("d1", 1, 0),
    ("d1", 2, 0), ("s3", 7), ("s3b", 7), ("s2b", 10), ("s4a", 3), ("s2a", 10), ("s2b", 8), ("s4a", 4),
    ("s2b", 9), ("s4c", 5), ("s4b", 3), ("s4b", 4), ("s4f2", 5), ("s2a", 8), ("s2b", 11), ("s3", 6), ("s3b", 6),
    ("s4f1", 3), ("s4a", 7), ("s4f1", 4), ("s2a", 11), ("s4b", 7), ("s3", 9), ("s4f2", 3), ("s3b", 9),
    ("s4f1", 7), ("s4f2", 4), ("s4c", 3), ("s4c", 4), ("s3", 10), ("s3b", 10), ("s4a", 6), ("s5", 5),
    ("d1", 4, 0), ("s4a", 9), ("s4b", 6), ("s4c", 7), ("s4f2", 7), ("s3", 8), ("s3b", 8), ("s4b", 9),
    ("s4a", 10), ("s4f1", 6), ("s5", 3), ("d1", 1, 1), ("s6", 1), ("s4b", 10), ("s4f2", 6), ("d3", 1),
    ("s4f1", 9), ("s3", 11), ("s4f2", 9), ("s4c", 6), ("s3b", 11), ("s4f1", 10), ("s5", 4), ("d1", 2, 1),
    ("d1", 3, 0), ("s5", 7), ("s6", 2), ("s4b", 8), ("s4f2", 10), ("d3", 2), ("s4c", 9), ("s4f1", 8),
    ("s4a", 8), ("s4c", 10), ("s5", 6), ("d1", 3, 1), ("d1", 4, 1), ("s6", 3), ("s4b", 11), ("s4f1", 11),
    ("s4a", 11), ("s5", 9), ("d1", 5, 1), ("d3", 3), ("d3", 4), ("s4c", 8), ("s5", 10), ("d1", 6, 1), ("d2", 5),
    ("s4f2", 8), ("d2", 6), ("s4f2", 11), ("s4c", 11), ("s5", 8), ("d1", 5, 0), ("d1", 6, 0), ("s6", 4),
    ("s5", 11), ("d1", 7, 1), ("d1", 7, 0), ("d3", 5), ("s6", 5), ("d2", 7), ("d3", 6), ("fin",), ("d2", 0),
    ("d3", 7), ("d4",),
)

OFFSETS = tuple(sum(CHUNKS[:i]) for i in range(len(CHUNKS)))
X_ROWS = sum(n for n, m in zip(CHUNKS, X_FIRST) if m)
Y_ROWS = sum(CHUNKS) - X_ROWS
SAME = tuple(
    sum(n for n, m in zip(CHUNKS[:i], X_FIRST) if m == X_FIRST[i]) for i in range(len(CHUNKS))
)
COPIES = 512


def dot(a, b, i, j):
    return lax.dot_general(a, b, (((i,), (j,)), ((), ())), preferred_element_type=F32)


class Sum:
    names = ("own", "s1y", "r1y", "s2x", "r2x", "s1x", "r1x", "s2y", "r2y", "fin")

    def __init__(self, refs):
        for name, ref in zip(self.names, refs):
            setattr(self, name, ref)
        self.first, self.second = {}, {}

    @staticmethod
    def shapes(columns, x_rows, y_rows):
        x, y = max(x_rows, 128), max(y_rows, 128)
        return [
            ((x_rows + y_rows, columns), F32),
            ((y // 2, columns), BF16), ((y // 2, columns), BF16),
            ((y // 2, columns), BF16), ((3, y // 8, columns), BF16),
            ((x, columns), BF16), ((3, 2, x // 8, columns), BF16),
            ((x // 8, columns), BF16), ((x // 8, columns), BF16), ((x // 8, columns), F32),
        ]


def kernel(tok_in, cot_in, gw_in, uw_in, dw_in, ig_out, gg_out, ug_out, dg_out, *scratch):
    act, wgu, dw = scratch[:3]
    gu, h = Sum(scratch[3:13]), Sum(scratch[13:23])
    (
        pa, pb, ip, d_r1, d_s2, d_r2, d_s3, d_r3, d_sz, d_rz,
        acc_gu, acc_d, ig_v, send_sem, recv_sem, local_sem,
    ) = scratch[23:]
    rows, units = tok_in.shape[0], gw_in.shape[0]
    z, gy, gz = lax.axis_index("gx"), lax.axis_index("gy"), lax.axis_index("gz")
    yh, core, x, yl = gy // 2, gy % 2, gz // 2, gz % 2
    sibling = (z, yh * 2 + (1 - core), gz)
    far = (z, (1 - yh) * 2 + core, gz)
    near = (z, gy, x * 2 + (1 - yl))

    def along_z(d):
        return (lax.rem(z + 8 + d, 8), gy, gz)

    def x_of(d):
        return lax.rem(x + d, 4)

    def along_x(d):
        return (z, gy, x_of(d) * 2 + yl)

    def at(start, n):
        return pl.ds(pl.multiple_of(start, 16), n)

    def place(d, half):
        return UNITS.index((d, half)) * 2 * rows

    copies, sent_act = [], []

    def send(src, dst, device):
        i = len(copies)
        copy = pltpu.make_async_remote_copy(
            src_ref=src, dst_ref=dst, send_sem=send_sem.at[i], recv_sem=recv_sem.at[i],
            device_id=device, device_id_type=pl.DeviceIdType.MESH,
        )
        copy.start()
        copies.append(copy)
        return copy

    locals_ = []

    def local(src, dst):
        copy = pltpu.make_async_copy(src, dst, local_sem.at[len(locals_)])
        copy.start()
        locals_.append(copy)
        return copy

    mine = pl.ds(place(0, 0), rows)
    own = [local(tok_in, act.at[0, mine]), local(cot_in, act.at[1, mine])]
    weights = [
        local(gw_in, wgu.at[pl.ds(0, units)]), local(uw_in, wgu.at[pl.ds(units, units)]), local(dw_in, dw)
    ]

    barrier = pltpu.get_barrier_semaphore()
    peers = [sibling, far, near] + [along_x(d) for d in (1, 2, 3)] + [along_z(d) for d in range(1, 8)]
    for peer in peers:
        pl.semaphore_signal(barrier, inc=1, device_id=peer, device_id_type=pl.DeviceIdType.MESH)
    pl.semaphore_wait(barrier, len(peers))

    got, sib = {}, {}

    def rows_at(d, half, other, which=None):
        span = pl.ds(place(d, half) + other * rows, rows)
        return act.at[:, span] if which is None else act.at[which, span]

    def ring(j, half):
        for sign in (1, -1):
            which = None if j < 4 else (0 if sign == 1 else 1)
            src, dst = -sign * (j - 1), (-sign * j if j < 4 else 4)
            got[sign, j, half] = send(
                rows_at(src, half, 0, which), rows_at(dst, half, 0, which), along_z(sign)
            )
            sent_act.append(got[sign, j, half])

    def to_sibling(d, half, which=None):
        sent_act.append(send(rows_at(d, half, 0, which), rows_at(d, half, 1, which), sibling))
        return sent_act[-1]

    waited = []

    def arrive(copy):
        if not any(copy is other for other in waited):
            waited.append(copy)
            copy.wait_recv()

    def a0():
        for copy in own:
            copy.wait()
        sib["far"] = send(rows_at(0, 0, 0), rows_at(0, 1, 0), far)
        sent_act.append(sib["far"])
        ring(1, 0)
        sib[0, 0] = [to_sibling(0, 0)]

    def a1():
        arrive(sib["far"])
        ring(1, 1)
        sib[0, 1] = [to_sibling(0, 1)]

    def forward(j, half):
        for sign in (1, -1):
            arrive(got[sign, j, half])
        if j < 4:
            ring(j + 1, half)
            for d in (j, -j):
                sib[d, half] = [to_sibling(d, half)]
        else:
            sib[4, half] = [to_sibling(4, half, 0), to_sibling(4, half, 1)]

    def ready(k):
        lo, hi = OFFSETS[k], OFFSETS[k] + CHUNKS[k]
        for i, unit in enumerate(UNITS):
            if i * 2 * rows < hi and (i + 1) * 2 * rows > lo:
                for copy in sib[unit]:
                    arrive(copy)
        for copy in weights:
            if not any(copy is other for other in waited):
                waited.append(copy)
                copy.wait()

    def sizes(k):
        return OFFSETS[k], CHUNKS[k], CHUNKS[k] // 2, CHUNKS[k] // 8

    def start_sum(a, k, x_first, term):
        o, n, q, r = sizes(k)
        a.own[pl.ds(o, n)] = term
        if x_first:
            a.s1x[pl.ds(SAME[k], n)] = term.astype(BF16)
            a.first[k] = [
                send(
                    a.s1x.at[at(SAME[k] + y * q + x_of(d) * r, r)],
                    a.r1x.at[d - 1, y, pl.ds(SAME[k] // 8, r)],
                    along_x(d),
                )
                for d in (1, 3, 2) for y in (0, 1)
            ]
        else:
            half = pl.ds(SAME[k] // 2, q)
            a.s1y[half] = a.own[at(o + (1 - yl) * q, q)].astype(BF16)
            a.first[k] = [send(a.s1y.at[half], a.r1y.at[half], near)]

    def go_on(a, k, x_first):
        o, n, q, r = sizes(k)
        half, piece = pl.ds(SAME[k] // 2, q), pl.ds(SAME[k] // 8, r)
        for copy in a.first[k]:
            arrive(copy)
        if x_first:
            def total(y):
                value = a.own[at(o + y * q + x * r, r)]
                for d in range(3):
                    value = value + a.r1x[d, y, piece].astype(F32)
                return value

            a.s2y[piece] = total(1 - yl).astype(BF16)
            a.second[k] = [send(a.s2y.at[piece], a.r2y.at[piece], near)]
            a.fin[piece] = total(yl)
        else:
            a.s2x[half] = (a.own[at(o + yl * q, q)] + a.r1y[half].astype(F32)).astype(BF16)
            a.second[k] = [
                send(a.s2x.at[at(SAME[k] // 2 + x_of(d) * r, r)], a.r2x.at[d - 1, piece], along_x(d))
                for d in (1, 3, 2)
            ]

    def end_sum(a, k, x_first):
        o, n, q, r = sizes(k)
        piece = pl.ds(SAME[k] // 8, r)
        for copy in a.second[k]:
            arrive(copy)
        if x_first:
            return a.fin[piece] + a.r2y[piece].astype(F32)
        value = a.own[at(o + yl * q + x * r, r)] + a.r1y[at(SAME[k] // 2 + x * r, r)].astype(F32)
        for d in range(3):
            value = value + a.r2x[d, piece].astype(F32)
        return value

    def s1a(k):
        ready(k)
        start_sum(gu, k, X_FIRST[k], dot(act[0, pl.ds(OFFSETS[k], CHUNKS[k])], wgu[...], 1, 1))

    def s1b(k):
        ready(k)
        start_sum(h, k, not X_FIRST[k], dot(act[1, pl.ds(OFFSETS[k], CHUNKS[k])], dw[...], 1, 1))

    def s2a(k):
        go_on(h if X_FIRST[k] else gu, k, False)

    def s2b(k):
        go_on(gu if X_FIRST[k] else h, k, True)

    pa_y, pa_x, pb_y, pb_x, pa_xx, pb_yy = {}, {}, {}, {}, {}, {}

    def rows_of(k, y, of):
        o, n, q, r = sizes(k)
        return at(o + y * q + of * r, r)

    def same(ref, span, device):
        return send(ref.at[span], ref.at[span], device)

    def ways(k):
        return (1, 3) if FORWARD[k] else (1, 3, 2)

    def s3(k):
        g = end_sum(gu, k, X_FIRST[k])
        hidden_grad = end_sum(h, k, not X_FIRST[k])
        gate, up = g[:, :units], g[:, units:]
        sigmoid_gate = jax.nn.sigmoid(gate)
        span = rows_of(k, yl, x)
        up_part = hidden_grad * gate * sigmoid_gate
        gate_part = hidden_grad * up * sigmoid_gate * (1.0 + gate * (1.0 - sigmoid_gate))
        pa[span] = jnp.concatenate([gate_part, up_part], axis=1).astype(BF16)
        pa_y[k] = same(pa, span, near)
        pa_x[k] = {d: same(pa, span, along_x(d)) for d in ways(k)}
        pb[span] = (gate * sigmoid_gate * up).astype(BF16)

    def s3b(k):
        span = rows_of(k, yl, x)
        pb_x[k] = {d: same(pb, span, along_x(d)) for d in ways(k)}
        pb_y[k] = same(pb, span, near)

    def s4a(k):
        arrive(pa_y[k])
        span = rows_of(k, 1 - yl, x)
        pa_xx[k] = {d: same(pa, span, along_x(d)) for d in ways(k)}

    def s4f1(k):
        arrive(pa_x[k][1])
        pa_x[k][2] = same(pa, rows_of(k, yl, x_of(3)), along_x(1))

    def s4f2(k):
        arrive(pa_xx[k][3])
        pa_xx[k][2] = same(pa, rows_of(k, 1 - yl, x_of(1)), along_x(3))

    def s4b(k):
        pb_yy[k] = []
        for d in ways(k):
            arrive(pb_x[k][d])
            pb_yy[k].append(same(pb, rows_of(k, yl, x_of(4 - d)), near))
        if FORWARD[k]:
            d = 1 if k % 2 else 3
            pb_x[k][2] = same(pb, rows_of(k, yl, x_of(4 - d)), along_x(d))

    def s4c(k):
        arrive(pb_x[k][2])
        pb_yy[k].append(same(pb, rows_of(k, yl, x_of(2)), near))

    def s5(k):
        for copy in (*pa_x[k].values(), *pa_xx[k].values()):
            arrive(copy)
        span = pl.ds(OFFSETS[k], CHUNKS[k])
        ip[span] = dot(pa[span], wgu[...], 1, 0)

    summed = []

    def s6(g):
        for k in GROUPS[g]:
            for copy in [pb_y[k]] + pb_yy[k]:
                arrive(copy)
        span = pl.ds(OFFSETS[GROUPS[g][0]], sum(CHUNKS[k] for k in GROUPS[g]))
        gu_term = dot(pa[span], act[0, span], 0, 0)
        acc_gu[...] = acc_gu[...] + gu_term if summed else gu_term
        d_term = dot(pb[span], act[1, span], 0, 0)
        acc_d[...] = acc_d[...] + d_term if summed else d_term
        summed.append(g)

    dc, dy, dz = {}, {}, {}

    def d1(s, half):
        start = place(SLOTS[s], half)
        dc[s, half] = send(ip.at[pl.ds(start + rows, rows)], d_r1.at[s, half], sibling)

    def both(s, half):
        arrive(dc[s, half])
        return ip[pl.ds(place(SLOTS[s], half), rows)] + d_r1[s, half]

    def d2(s):
        value = both(s, 1)
        if s == 0:
            for i, d in enumerate(NEAR_Z):
                arrive(dz[SLOTS.index(d)])
                value = value + d_rz[i, 1].astype(F32)
        d_s2[s] = value.astype(BF16)
        dy[s] = send(d_s2.at[s], d_r2.at[s], far)

    def d3(s):
        if SLOTS[s] in NEAR_Z:
            i = NEAR_Z.index(SLOTS[s])
            for half in (0, 1):
                d_sz[i, half] = both(s, half).astype(BF16)
            dz[s] = send(d_sz.at[i], d_rz.at[i], along_z(SLOTS[s]))
        else:
            value = both(s, 0)
            arrive(dy[s])
            d_s3[s] = (value + d_r2[s].astype(F32)).astype(BF16)
            dz[s] = send(d_s3.at[s], d_r3.at[s - 1], along_z(SLOTS[s]))

    outs = []

    def d4():
        value = both(0, 0)
        arrive(dy[0])
        value = value + d_r2[0].astype(F32)
        for s in range(1, 8):
            arrive(dz[s])
            if SLOTS[s] in NEAR_Z:
                value = value + d_rz[NEAR_Z.index(SLOTS[s]), 0].astype(F32)
            else:
                value = value + d_r3[s - 1].astype(F32)
        ig_v[...] = value.astype(BF16)
        outs.append(local(ig_v, ig_out))

    def fin():
        for copy in sent_act:
            copy.wait_send()
        first, second = pl.ds(0, units), pl.ds(units, units)
        act[0, pl.ds(0, 2 * units)] = acc_gu[...].astype(BF16)
        outs.append(local(act.at[0, first], gg_out))
        outs.append(local(act.at[0, second], ug_out))
        act[1, first] = acc_d[...].astype(BF16)
        outs.append(local(act.at[1, first], dg_out))

    steps = {
        "A0": a0, "A1": a1, "R": forward, "s1a": s1a, "s1b": s1b, "s2a": s2a, "s2b": s2b, "s3": s3, "s3b": s3b,
        "s4a": s4a, "s4f1": s4f1, "s4f2": s4f2, "s4b": s4b, "s4c": s4c, "s5": s5, "s6": s6,
        "d1": d1, "d2": d2, "d3": d3, "d4": d4, "fin": fin,
    }
    for name, *where in ORDER:
        steps[name](*where)
    for copy in copies:
        if not any(copy is other for other in sent_act):
            copy.wait_send()
    for copy in outs:
        copy.wait()


def on_device(tokens, cotangent, gate_weight, up_weight, down_weight):
    rows, width = tokens.shape
    units = down_weight.shape[0]
    n = rows * 32
    scratch = [
        ((2, n, width), BF16), ((2 * units, width), BF16), ((units, width), BF16),
        *Sum.shapes(2 * units, X_ROWS, Y_ROWS), *Sum.shapes(units, Y_ROWS, X_ROWS),
        ((n, 2 * units), BF16), ((n, units), BF16), ((n, width), F32),
        ((8, 2, rows, width), F32), ((8, rows, width), BF16), ((8, rows, width), BF16),
        ((8, rows, width), BF16), ((7, rows, width), BF16),
        ((max(len(NEAR_Z), 1), 2, rows, width), BF16), ((max(len(NEAR_Z), 1), 2, rows, width), BF16),
        ((2 * units, width), F32), ((units, width), F32),
        ((rows, width), BF16),
    ]
    input_grad, gate_grad, up_grad, down_grad = pl.pallas_call(
        kernel,
        out_shape=[
            jax.ShapeDtypeStruct(a.shape, BF16) for a in (tokens, down_weight, down_weight, down_weight)
        ],
        in_specs=[pl.BlockSpec(memory_space=pl.ANY)] * 5,
        out_specs=[pl.BlockSpec(memory_space=pl.ANY)] * 4,
        scratch_shapes=[pltpu.VMEM(shape, dtype) for shape, dtype in scratch]
        + [
            pltpu.SemaphoreType.DMA((COPIES,)),
            pltpu.SemaphoreType.DMA((COPIES,)),
            pltpu.SemaphoreType.DMA((16,)),
        ],
        compiler_params=pltpu.CompilerParams(
            collective_id=0, has_side_effects=True, vmem_limit_bytes=61 * 2**20
        ),
        cost_estimate=pl.CostEstimate(
            flops=16 * n * width * units, bytes_accessed=6 * 2**20, transcendentals=n * units // 8
        ),
    )(tokens, cotangent, gate_weight.T, up_weight.T, down_weight)
    return input_grad, gate_grad.T, up_grad.T, down_grad


def solution(mesh):
    blocks = ("gx", "gy")
    by_row, by_column = P(blocks, "gz"), P("gz", blocks)
    return jax.shard_map(
        on_device,
        mesh=mesh,
        in_specs=(by_row, by_row, by_column, by_column, by_row),
        out_specs=(by_row, by_column, by_column, by_row),
        check_vma=False,
    )
```

```python
import jax
import jax.numpy as jnp
from jax import lax
from jax.experimental import pallas as pl
from jax.experimental.pallas import tpu as pltpu
from jax.sharding import PartitionSpec as P

F32, BF16 = jnp.float32, jnp.bfloat16
SLOTS = (0, 1, -1, 2, -2, 3, -3, 4)
UNITS = ((0, 0), (0, 1), (1, 0), (-1, 0), (1, 1), (-1, 1), (2, 0), (-2, 0), (2, 1), (-2, 1), (3, 0), (-3, 0), (3, 1), (-3, 1), (4, 0), (4, 1))
CHUNKS = (128, 128, 128, 128, 128, 128, 128, 128, 128, 128, 128, 128)
X_FIRST = (True, False, False, False, False, True, False, True, False, True, False, False)
FORWARD = (True, False, True, True, True, True, True, True, True, True, True, True)
GROUPS = ((0, 1), (2, 3), (4, 5), (6, 7), (8, 9), (10, 11))
NEAR_Z = (1, -1, 2, -2)
ORDER = (
    ("A0",), ("R", 1, 0), ("A1",), ("s1a", 2), ("s1a", 0), ("s1a", 1), ("s1b", 0), ("s1b", 1), ("s1b", 2),
    ("s2a", 0), ("s2b", 1), ("s2a", 2), ("s2b", 2), ("R", 2, 0), ("s2b", 0), ("s2a", 1), ("R", 1, 1),
    ("s1a", 5), ("s1b", 5), ("s1a", 3), ("s1a", 4), ("s1b", 3), ("s1b", 4), ("s3", 0), ("s3b", 0), ("s3", 2),
    ("s3b", 2), ("s3", 1), ("s3b", 1), ("s2a", 5), ("R", 3, 0), ("s2b", 3), ("s4a", 0), ("R", 2, 1), ("s2b", 4),
    ("s4b", 0), ("s2b", 5), ("s4b", 2), ("s4a", 2), ("s1a", 6), ("s1a", 7), ("s4f1", 0), ("s1b", 6), ("s1b", 7),
    ("s4f1", 2), ("s2a", 3), ("s2a", 4), ("s4a", 1), ("s4b", 1), ("s4c", 0), ("s4f2", 0), ("s4c", 2),
    ("R", 4, 0), ("s3", 5), ("s3b", 5), ("s4f2", 2), ("R", 3, 1), ("s1a", 9), ("s2a", 7), ("s1a", 10),
    ("s2b", 6), ("s1b", 9), ("s1b", 10), ("s4a", 5), ("s2a", 6), ("s1a", 8), ("s1b", 8), ("s2b", 7),
    ("R", 4, 1), ("s3", 3), ("s4b", 5), ("s3b", 3), ("s3", 4), ("s3b", 4), ("s1a", 11), ("s1b", 11), ("s5", 0),
    ("d1", 0, 0), ("s5", 1), ("d1", 0, 1), ("s6", 0), ("s4f1", 5), ("s2a", 9), ("s5", 2), ("d1", 1, 0),
    ("d1", 2, 0), ("s3", 7), ("s3b", 7), ("s2b", 10), ("s4a", 3), ("s2a", 10), ("s2b", 8), ("s4a", 4),
    ("s2b", 9), ("s4c", 5), ("s4b", 3), ("s4b", 4), ("s4f2", 5), ("s2a", 8), ("s2b", 11), ("s3", 6), ("s3b", 6),
    ("s4f1", 3), ("s4a", 7), ("s4f1", 4), ("s2a", 11), ("s4b", 7), ("s3", 9), ("s4f2", 3), ("s3b", 9),
    ("s4f1", 7), ("s4f2", 4), ("s4c", 3), ("s4c", 4), ("s3", 10), ("s3b", 10), ("s4a", 6), ("s5", 5),
    ("d1", 4, 0), ("s4a", 9), ("s4b", 6), ("s4c", 7), ("s4f2", 7), ("s3", 8), ("s3b", 8), ("s4b", 9),
    ("s4a", 10), ("s4f1", 6), ("s5", 3), ("d1", 1, 1), ("s6", 1), ("s4b", 10), ("s4f2", 6), ("d3", 1),
    ("s4f1", 9), ("s3", 11), ("s4f2", 9), ("s4c", 6), ("s4f1", 10), ("s3b", 11), ("s5", 4), ("d1", 2, 1),
    ("d1", 3, 0), ("s6", 2), ("s4b", 8), ("s4a", 8), ("s5", 7), ("s4f2", 10), ("d3", 2), ("s4c", 9),
    ("s4f1", 8), ("s4c", 10), ("s5", 6), ("d1", 3, 1), ("d1", 4, 1), ("s6", 3), ("s4b", 11), ("s4f1", 11),
    ("s4a", 11), ("s5", 9), ("d1", 5, 1), ("d3", 3), ("d3", 4), ("s4c", 8), ("s4f2", 8), ("s5", 10),
    ("d1", 6, 1), ("d2", 5), ("d2", 6), ("s4f2", 11), ("s4c", 11), ("s5", 8), ("d1", 5, 0), ("d1", 6, 0),
    ("s6", 4), ("s5", 11), ("d1", 7, 1), ("d1", 7, 0), ("d3", 5), ("s6", 5), ("d2", 7), ("d3", 6), ("fin",),
    ("d2", 0), ("d3", 7), ("d4",),
)

OFFSETS = tuple(sum(CHUNKS[:i]) for i in range(len(CHUNKS)))
X_ROWS = sum(n for n, m in zip(CHUNKS, X_FIRST) if m)
Y_ROWS = sum(CHUNKS) - X_ROWS
SAME = tuple(
    sum(n for n, m in zip(CHUNKS[:i], X_FIRST) if m == X_FIRST[i]) for i in range(len(CHUNKS))
)
COPIES = 512


def dot(a, b, i, j):
    return lax.dot_general(a, b, (((i,), (j,)), ((), ())), preferred_element_type=F32)


class Sum:
    names = ("own", "s1y", "r1y", "s2x", "r2x", "s1x", "r1x", "s2y", "r2y", "fin")

    def __init__(self, refs):
        for name, ref in zip(self.names, refs):
            setattr(self, name, ref)
        self.first, self.second = {}, {}

    @staticmethod
    def shapes(columns, x_rows, y_rows):
        x, y = max(x_rows, 128), max(y_rows, 128)
        return [
            ((x_rows + y_rows, columns), F32),
            ((y // 2, columns), BF16), ((y // 2, columns), BF16),
            ((y // 2, columns), BF16), ((3, y // 8, columns), BF16),
            ((x, columns), BF16), ((3, 2, x // 8, columns), BF16),
            ((x // 8, columns), BF16), ((x // 8, columns), BF16), ((x // 8, columns), F32),
        ]


def kernel(tok_in, cot_in, gw_in, uw_in, dw_in, ig_out, gg_out, ug_out, dg_out, *scratch):
    act, wgu, dw = scratch[:3]
    gu, h = Sum(scratch[3:13]), Sum(scratch[13:23])
    (
        pa, pb, ip, d_r1, d_s2, d_r2, d_s3, d_r3, d_sz, d_rz,
        acc_gu, acc_d, ig_v, wt, dt, send_sem, recv_sem, local_sem,
    ) = scratch[23:]
    rows, units = tok_in.shape[0], gw_in.shape[0]
    z, gy, gz = lax.axis_index("gx"), lax.axis_index("gy"), lax.axis_index("gz")
    yh, core, x, yl = gy // 2, gy % 2, gz // 2, gz % 2
    sibling = (z, yh * 2 + (1 - core), gz)
    far = (z, (1 - yh) * 2 + core, gz)
    near = (z, gy, x * 2 + (1 - yl))

    def along_z(d):
        return (lax.rem(z + 8 + d, 8), gy, gz)

    def x_of(d):
        return lax.rem(x + d, 4)

    def along_x(d):
        return (z, gy, x_of(d) * 2 + yl)

    def at(start, n):
        return pl.ds(pl.multiple_of(start, 16), n)

    def place(d, half):
        return UNITS.index((d, half)) * 2 * rows

    copies, sent_act = [], []

    def send(src, dst, device):
        i = len(copies)
        copy = pltpu.make_async_remote_copy(
            src_ref=src, dst_ref=dst, send_sem=send_sem.at[i], recv_sem=recv_sem.at[i],
            device_id=device, device_id_type=pl.DeviceIdType.MESH,
        )
        copy.start()
        copies.append(copy)
        return copy

    locals_ = []

    def local(src, dst):
        copy = pltpu.make_async_copy(src, dst, local_sem.at[len(locals_)])
        copy.start()
        locals_.append(copy)
        return copy

    mine = pl.ds(place(0, 0), rows)
    own = [local(tok_in, act.at[0, mine]), local(cot_in, act.at[1, mine])]
    weights = [
        local(gw_in, wgu.at[pl.ds(0, units)]), local(uw_in, wgu.at[pl.ds(units, units)]), local(dw_in, dw)
    ]

    barrier = pltpu.get_barrier_semaphore()
    peers = [sibling, far, near] + [along_x(d) for d in (1, 2, 3)] + [along_z(d) for d in range(1, 8)]
    for peer in peers:
        pl.semaphore_signal(barrier, inc=1, device_id=peer, device_id_type=pl.DeviceIdType.MESH)
    pl.semaphore_wait(barrier, len(peers))

    got, sib = {}, {}

    def rows_at(d, half, other, which=None):
        span = pl.ds(place(d, half) + other * rows, rows)
        return act.at[:, span] if which is None else act.at[which, span]

    def ring(j, half):
        for sign in (1, -1):
            which = None if j < 4 else (0 if sign == 1 else 1)
            src, dst = -sign * (j - 1), (-sign * j if j < 4 else 4)
            got[sign, j, half] = send(
                rows_at(src, half, 0, which), rows_at(dst, half, 0, which), along_z(sign)
            )
            sent_act.append(got[sign, j, half])

    def to_sibling(d, half, which=None):
        sent_act.append(send(rows_at(d, half, 0, which), rows_at(d, half, 1, which), sibling))
        return sent_act[-1]

    waited = []

    def arrive(copy):
        if not any(copy is other for other in waited):
            waited.append(copy)
            copy.wait_recv()

    def a0():
        for copy in own:
            copy.wait()
        sib["far"] = send(rows_at(0, 0, 0), rows_at(0, 1, 0), far)
        sent_act.append(sib["far"])
        ring(1, 0)
        sib[0, 0] = [to_sibling(0, 0)]
        for copy in weights:
            copy.wait()
        wt[...] = wgu[...].T
        dt[...] = dw[...].T

    def a1():
        arrive(sib["far"])
        ring(1, 1)
        sib[0, 1] = [to_sibling(0, 1)]

    def forward(j, half):
        for sign in (1, -1):
            arrive(got[sign, j, half])
        if j < 4:
            ring(j + 1, half)
            for d in (j, -j):
                sib[d, half] = [to_sibling(d, half)]
        else:
            sib[4, half] = [to_sibling(4, half, 0), to_sibling(4, half, 1)]

    def ready(k):
        lo, hi = OFFSETS[k], OFFSETS[k] + CHUNKS[k]
        for i, unit in enumerate(UNITS):
            if i * 2 * rows < hi and (i + 1) * 2 * rows > lo:
                for copy in sib[unit]:
                    arrive(copy)

    def sizes(k):
        return OFFSETS[k], CHUNKS[k], CHUNKS[k] // 2, CHUNKS[k] // 8

    def start_sum(a, k, x_first, term):
        o, n, q, r = sizes(k)
        a.own[pl.ds(o, n)] = term
        if x_first:
            a.s1x[pl.ds(SAME[k], n)] = term.astype(BF16)
            a.first[k] = [
                send(
                    a.s1x.at[at(SAME[k] + y * q + x_of(d) * r, r)],
                    a.r1x.at[d - 1, y, pl.ds(SAME[k] // 8, r)],
                    along_x(d),
                )
                for d in (1, 3, 2) for y in (0, 1)
            ]
        else:
            half = pl.ds(SAME[k] // 2, q)
            a.s1y[half] = a.own[at(o + (1 - yl) * q, q)].astype(BF16)
            a.first[k] = [send(a.s1y.at[half], a.r1y.at[half], near)]

    def go_on(a, k, x_first):
        o, n, q, r = sizes(k)
        half, piece = pl.ds(SAME[k] // 2, q), pl.ds(SAME[k] // 8, r)
        for copy in a.first[k]:
            arrive(copy)
        if x_first:
            def total(y):
                value = a.own[at(o + y * q + x * r, r)]
                for d in range(3):
                    value = value + a.r1x[d, y, piece].astype(F32)
                return value

            a.s2y[piece] = total(1 - yl).astype(BF16)
            a.second[k] = [send(a.s2y.at[piece], a.r2y.at[piece], near)]
            a.fin[piece] = total(yl)
        else:
            a.s2x[half] = (a.own[at(o + yl * q, q)] + a.r1y[half].astype(F32)).astype(BF16)
            a.second[k] = [
                send(a.s2x.at[at(SAME[k] // 2 + x_of(d) * r, r)], a.r2x.at[d - 1, piece], along_x(d))
                for d in (1, 3, 2)
            ]

    def end_sum(a, k, x_first):
        o, n, q, r = sizes(k)
        piece = pl.ds(SAME[k] // 8, r)
        for copy in a.second[k]:
            arrive(copy)
        if x_first:
            return a.fin[piece] + a.r2y[piece].astype(F32)
        value = a.own[at(o + yl * q + x * r, r)] + a.r1y[at(SAME[k] // 2 + x * r, r)].astype(F32)
        for d in range(3):
            value = value + a.r2x[d, piece].astype(F32)
        return value

    def s1a(k):
        ready(k)
        start_sum(gu, k, X_FIRST[k], dot(act[0, pl.ds(OFFSETS[k], CHUNKS[k])], wt[...], 1, 0))

    def s1b(k):
        ready(k)
        start_sum(h, k, not X_FIRST[k], dot(act[1, pl.ds(OFFSETS[k], CHUNKS[k])], dt[...], 1, 0))

    def s2a(k):
        go_on(h if X_FIRST[k] else gu, k, False)

    def s2b(k):
        go_on(gu if X_FIRST[k] else h, k, True)

    pa_y, pa_x, pb_y, pb_x, pa_xx, pb_yy = {}, {}, {}, {}, {}, {}

    def rows_of(k, y, of):
        o, n, q, r = sizes(k)
        return at(o + y * q + of * r, r)

    def same(ref, span, device):
        return send(ref.at[span], ref.at[span], device)

    def ways(k):
        return (1, 3) if FORWARD[k] else (1, 3, 2)

    def s3(k):
        g = end_sum(gu, k, X_FIRST[k])
        hidden_grad = end_sum(h, k, not X_FIRST[k])
        gate, up = g[:, :units], g[:, units:]
        sigmoid_gate = jax.nn.sigmoid(gate)
        span = rows_of(k, yl, x)
        up_part = hidden_grad * gate * sigmoid_gate
        gate_part = hidden_grad * up * sigmoid_gate * (1.0 + gate * (1.0 - sigmoid_gate))
        pa[span] = jnp.concatenate([gate_part, up_part], axis=1).astype(BF16)
        pa_y[k] = same(pa, span, near)
        pa_x[k] = {d: same(pa, span, along_x(d)) for d in ways(k)}
        pb[span] = (gate * sigmoid_gate * up).astype(BF16)

    def s3b(k):
        span = rows_of(k, yl, x)
        pb_x[k] = {d: same(pb, span, along_x(d)) for d in ways(k)}
        pb_y[k] = same(pb, span, near)

    def s4a(k):
        arrive(pa_y[k])
        span = rows_of(k, 1 - yl, x)
        pa_xx[k] = {d: same(pa, span, along_x(d)) for d in ways(k)}

    def s4f1(k):
        arrive(pa_x[k][1])
        pa_x[k][2] = same(pa, rows_of(k, yl, x_of(3)), along_x(1))

    def s4f2(k):
        arrive(pa_xx[k][3])
        pa_xx[k][2] = same(pa, rows_of(k, 1 - yl, x_of(1)), along_x(3))

    def s4b(k):
        pb_yy[k] = []
        for d in ways(k):
            arrive(pb_x[k][d])
            pb_yy[k].append(same(pb, rows_of(k, yl, x_of(4 - d)), near))
        if FORWARD[k]:
            d = 1 if k % 2 else 3
            pb_x[k][2] = same(pb, rows_of(k, yl, x_of(4 - d)), along_x(d))

    def s4c(k):
        arrive(pb_x[k][2])
        pb_yy[k].append(same(pb, rows_of(k, yl, x_of(2)), near))

    def s5(k):
        for copy in (*pa_x[k].values(), *pa_xx[k].values()):
            arrive(copy)
        span = pl.ds(OFFSETS[k], CHUNKS[k])
        ip[span] = dot(pa[span], wgu[...], 1, 0)

    summed = []

    def s6(g):
        for k in GROUPS[g]:
            for copy in [pb_y[k]] + pb_yy[k]:
                arrive(copy)
        span = pl.ds(OFFSETS[GROUPS[g][0]], sum(CHUNKS[k] for k in GROUPS[g]))
        gu_term = dot(pa[span], act[0, span], 0, 0)
        acc_gu[...] = acc_gu[...] + gu_term if summed else gu_term
        d_term = dot(pb[span], act[1, span], 0, 0)
        acc_d[...] = acc_d[...] + d_term if summed else d_term
        summed.append(g)

    dc, dy, dz = {}, {}, {}

    def d1(s, half):
        start = place(SLOTS[s], half)
        dc[s, half] = send(ip.at[pl.ds(start + rows, rows)], d_r1.at[s, half], sibling)

    def both(s, half):
        arrive(dc[s, half])
        return ip[pl.ds(place(SLOTS[s], half), rows)] + d_r1[s, half]

    def d2(s):
        value = both(s, 1)
        if s == 0:
            for i, d in enumerate(NEAR_Z):
                arrive(dz[SLOTS.index(d)])
                value = value + d_rz[i, 1].astype(F32)
        d_s2[s] = value.astype(BF16)
        dy[s] = send(d_s2.at[s], d_r2.at[s], far)

    def d3(s):
        if SLOTS[s] in NEAR_Z:
            i = NEAR_Z.index(SLOTS[s])
            for half in (0, 1):
                d_sz[i, half] = both(s, half).astype(BF16)
            dz[s] = send(d_sz.at[i], d_rz.at[i], along_z(SLOTS[s]))
        else:
            value = both(s, 0)
            arrive(dy[s])
            d_s3[s] = (value + d_r2[s].astype(F32)).astype(BF16)
            dz[s] = send(d_s3.at[s], d_r3.at[s - 1], along_z(SLOTS[s]))

    outs = []

    def d4():
        value = both(0, 0)
        arrive(dy[0])
        value = value + d_r2[0].astype(F32)
        for s in range(1, 8):
            arrive(dz[s])
            if SLOTS[s] in NEAR_Z:
                value = value + d_rz[NEAR_Z.index(SLOTS[s]), 0].astype(F32)
            else:
                value = value + d_r3[s - 1].astype(F32)
        ig_v[...] = value.astype(BF16)
        outs.append(local(ig_v, ig_out))

    def fin():
        for copy in sent_act:
            copy.wait_send()
        first, second = pl.ds(0, units), pl.ds(units, units)
        act[0, pl.ds(0, 2 * units)] = acc_gu[...].astype(BF16)
        outs.append(local(act.at[0, first], gg_out))
        outs.append(local(act.at[0, second], ug_out))
        act[1, first] = acc_d[...].astype(BF16)
        outs.append(local(act.at[1, first], dg_out))

    steps = {
        "A0": a0, "A1": a1, "R": forward, "s1a": s1a, "s1b": s1b, "s2a": s2a, "s2b": s2b, "s3": s3, "s3b": s3b,
        "s4a": s4a, "s4f1": s4f1, "s4f2": s4f2, "s4b": s4b, "s4c": s4c, "s5": s5, "s6": s6,
        "d1": d1, "d2": d2, "d3": d3, "d4": d4, "fin": fin,
    }
    for name, *where in ORDER:
        steps[name](*where)
    for copy in copies:
        if not any(copy is other for other in sent_act):
            copy.wait_send()
    for copy in outs:
        copy.wait()


def hand_over(*refs):
    n = len(refs) // 2
    for i in range(n):
        refs[n + i][...] = refs[i][...]


def on_device(tokens, cotangent, gate_weight, up_weight, down_weight):
    rows, width = tokens.shape
    units = down_weight.shape[0]
    n = rows * 32
    scratch = [
        ((2, n, width), BF16), ((2 * units, width), BF16), ((units, width), BF16),
        *Sum.shapes(2 * units, X_ROWS, Y_ROWS), *Sum.shapes(units, Y_ROWS, X_ROWS),
        ((n, 2 * units), BF16), ((n, units), BF16), ((n, width), F32),
        ((8, 2, rows, width), F32), ((8, rows, width), BF16), ((8, rows, width), BF16),
        ((8, rows, width), BF16), ((7, rows, width), BF16),
        ((max(len(NEAR_Z), 1), 2, rows, width), BF16), ((max(len(NEAR_Z), 1), 2, rows, width), BF16),
        ((2 * units, width), F32), ((units, width), F32),
        ((rows, width), BF16), ((width, 2 * units), BF16), ((width, units), BF16),
    ]
    results = [
        jax.ShapeDtypeStruct(a.shape, BF16) for a in (tokens, down_weight, down_weight, down_weight)
    ]
    values = pl.pallas_call(
        kernel,
        out_shape=results,
        in_specs=[pl.BlockSpec(memory_space=pl.ANY)] * 5,
        out_specs=[pl.BlockSpec(memory_space=pl.ANY)] * 4,
        scratch_shapes=[pltpu.VMEM(shape, dtype) for shape, dtype in scratch]
        + [
            pltpu.SemaphoreType.DMA((COPIES,)),
            pltpu.SemaphoreType.DMA((COPIES,)),
            pltpu.SemaphoreType.DMA((16,)),
        ],
        compiler_params=pltpu.CompilerParams(
            collective_id=0, has_side_effects=True, vmem_limit_bytes=61 * 2**20
        ),
        cost_estimate=pl.CostEstimate(
            flops=16 * n * width * units, bytes_accessed=6 * 2**20, transcendentals=n * units // 8
        ),
    )(tokens, cotangent, gate_weight.T, up_weight.T, down_weight)
    input_grad, gate_grad, up_grad, down_grad = pl.pallas_call(
        hand_over,
        out_shape=results,
    )(*values)
    return input_grad, gate_grad.T, up_grad.T, down_grad


def solution(mesh):
    blocks = ("gx", "gy")
    by_row, by_column = P(blocks, "gz"), P("gz", blocks)
    return jax.shard_map(
        on_device,
        mesh=mesh,
        in_specs=(by_row, by_row, by_column, by_column, by_row),
        out_specs=(by_row, by_column, by_column, by_row),
        check_vma=False,
    )
```

```python
import jax
import jax.numpy as jnp
from jax import lax
from jax.experimental import pallas as pl
from jax.experimental.pallas import tpu as pltpu
from jax.sharding import PartitionSpec as P

F32, BF16 = jnp.float32, jnp.bfloat16
SLOTS = (0, 1, -1, 2, -2, 3, -3, 4)
UNITS = ((0, 0), (0, 1), (1, 0), (-1, 0), (1, 1), (-1, 1), (2, 0), (-2, 0), (2, 1), (-2, 1), (3, 0), (-3, 0), (3, 1), (-3, 1), (4, 0), (4, 1))
CHUNKS = (128, 128, 128, 128, 128, 128, 128, 128, 128, 128, 128, 128)
X_FIRST = (True, False, False, False, False, True, False, True, False, True, False, False)
FORWARD = (True, False, True, True, True, True, True, True, True, True, True, True)
GROUPS = ((0, 1), (2, 3), (4, 5), (6, 7), (8, 9), (10, 11))
NEAR_Z = (1, -1, 2, -2)
ORDER = (
    ("A0",), ("R", 1, 0), ("A1",), ("s1a", 2), ("s1a", 0), ("s1a", 1), ("s1b", 0), ("s1b", 1), ("s1b", 2),
    ("s2a", 0), ("s2b", 1), ("s2a", 2), ("s2b", 2), ("R", 2, 0), ("s2b", 0), ("s2a", 1), ("R", 1, 1),
    ("s1a", 5), ("s1b", 5), ("s1a", 3), ("s1a", 4), ("s1b", 3), ("s1b", 4), ("s3", 0), ("s3b", 0), ("s3", 2),
    ("s3b", 2), ("s3", 1), ("s3b", 1), ("s2a", 5), ("R", 3, 0), ("s2b", 3), ("s4a", 0), ("R", 2, 1), ("s2b", 4),
    ("s4b", 0), ("s2b", 5), ("s4b", 2), ("s4a", 2), ("s1a", 6), ("s1a", 7), ("s4f1", 0), ("s1b", 6), ("s1b", 7),
    ("s4f1", 2), ("s2a", 3), ("s2a", 4), ("s4a", 1), ("s4b", 1), ("s4c", 0), ("s4f2", 0), ("s4c", 2),
    ("R", 4, 0), ("s3", 5), ("s3b", 5), ("s4f2", 2), ("R", 3, 1), ("s1a", 9), ("s2a", 7), ("s1a", 10),
    ("s2b", 6), ("s1b", 9), ("s1b", 10), ("s4a", 5), ("s2a", 6), ("s1a", 8), ("s1b", 8), ("s2b", 7),
    ("R", 4, 1), ("s3", 3), ("s4b", 5), ("s3b", 3), ("s3", 4), ("s3b", 4), ("s1a", 11), ("s1b", 11), ("s5", 0),
    ("d1", 0, 0), ("s5", 1), ("d1", 0, 1), ("s6", 0), ("s4f1", 5), ("s2a", 9), ("s5", 2), ("d1", 1, 0),
    ("d1", 2, 0), ("s3", 7), ("s3b", 7), ("s2b", 10), ("s4a", 3), ("s2a", 10), ("s2b", 8), ("s4a", 4),
    ("s2b", 9), ("s4c", 5), ("s4b", 3), ("s4b", 4), ("s4f2", 5), ("s2a", 8), ("s2b", 11), ("s3", 6), ("s3b", 6),
    ("s4f1", 3), ("s4a", 7), ("s4f1", 4), ("s2a", 11), ("s4b", 7), ("s3", 9), ("s4f2", 3), ("s3b", 9),
    ("s4f1", 7), ("s4f2", 4), ("s4c", 3), ("s4c", 4), ("s3", 10), ("s3b", 10), ("s4a", 6), ("s5", 5),
    ("d1", 4, 0), ("s4a", 9), ("s4b", 6), ("s4c", 7), ("s4f2", 7), ("s3", 8), ("s3b", 8), ("s4b", 9),
    ("s4a", 10), ("s4f1", 6), ("s5", 3), ("d1", 1, 1), ("s6", 1), ("s4b", 10), ("s4f2", 6), ("d3", 1),
    ("s4f1", 9), ("s3", 11), ("s4f2", 9), ("s4c", 6), ("s4f1", 10), ("s3b", 11), ("s5", 4), ("d1", 2, 1),
    ("d1", 3, 0), ("s6", 2), ("s4b", 8), ("s4a", 8), ("s5", 7), ("s4f2", 10), ("d3", 2), ("s4c", 9),
    ("s4f1", 8), ("s4c", 10), ("s5", 6), ("d1", 3, 1), ("d1", 4, 1), ("s6", 3), ("s4b", 11), ("s4f1", 11),
    ("s4a", 11), ("s5", 9), ("d1", 5, 1), ("d3", 3), ("d3", 4), ("s4c", 8), ("s4f2", 8), ("s5", 10),
    ("d1", 6, 1), ("d2", 5), ("d2", 6), ("s4f2", 11), ("s4c", 11), ("s5", 8), ("d1", 5, 0), ("d1", 6, 0),
    ("s6", 4), ("s5", 11), ("d1", 7, 1), ("d1", 7, 0), ("d3", 5), ("s6", 5), ("d2", 7), ("d3", 6), ("fin",),
    ("d2", 0), ("d3", 7), ("d4",),
)

OFFSETS = tuple(sum(CHUNKS[:i]) for i in range(len(CHUNKS)))
X_ROWS = sum(n for n, m in zip(CHUNKS, X_FIRST) if m)
Y_ROWS = sum(CHUNKS) - X_ROWS
SAME = tuple(
    sum(n for n, m in zip(CHUNKS[:i], X_FIRST) if m == X_FIRST[i]) for i in range(len(CHUNKS))
)
COPIES = 512


def dot(a, b, i, j):
    return lax.dot_general(a, b, (((i,), (j,)), ((), ())), preferred_element_type=F32)


class Sum:
    names = ("own", "s1y", "r1y", "s2x", "r2x", "s1x", "r1x", "s2y", "r2y", "fin")

    def __init__(self, refs):
        for name, ref in zip(self.names, refs):
            setattr(self, name, ref)
        self.first, self.second = {}, {}

    @staticmethod
    def shapes(columns, x_rows, y_rows):
        x, y = max(x_rows, 128), max(y_rows, 128)
        return [
            ((x_rows + y_rows, columns), F32),
            ((y // 2, columns), BF16), ((y // 2, columns), BF16),
            ((y // 2, columns), BF16), ((3, y // 8, columns), BF16),
            ((2, x // 2, columns), BF16), ((3, 2, x // 8, columns), BF16),
            ((x // 8, columns), BF16), ((x // 8, columns), BF16), ((x // 8, columns), F32),
        ]


def kernel(tok_in, cot_in, gw_in, uw_in, dw_in, ig_out, gg_out, ug_out, dg_out, *scratch):
    act, wgu, dw = scratch[:3]
    gu, h = Sum(scratch[3:13]), Sum(scratch[13:23])
    (
        pa, pb, ip, d_r1, d_s2, d_r2, d_s3, d_r3, d_sz, d_rz,
        acc_gu, acc_d, ig_v, wt, dt, send_sem, recv_sem, local_sem,
    ) = scratch[23:]
    rows, units = tok_in.shape[0], gw_in.shape[0]
    z, gy, gz = lax.axis_index("gx"), lax.axis_index("gy"), lax.axis_index("gz")
    yh, core, x, yl = gy // 2, gy % 2, gz // 2, gz % 2
    sibling = (z, yh * 2 + (1 - core), gz)
    far = (z, (1 - yh) * 2 + core, gz)
    near = (z, gy, x * 2 + (1 - yl))

    def along_z(d):
        return (lax.rem(z + 8 + d, 8), gy, gz)

    def x_of(d):
        return lax.rem(x + d, 4)

    def along_x(d):
        return (z, gy, x_of(d) * 2 + yl)

    def at(start, n):
        return pl.ds(pl.multiple_of(start, 16), n)

    def place(d, half):
        return UNITS.index((d, half)) * 2 * rows

    copies, sent_act = [], []

    def send(src, dst, device):
        i = len(copies)
        copy = pltpu.make_async_remote_copy(
            src_ref=src, dst_ref=dst, send_sem=send_sem.at[i], recv_sem=recv_sem.at[i],
            device_id=device, device_id_type=pl.DeviceIdType.MESH,
        )
        copy.start()
        copies.append(copy)
        return copy

    locals_ = []

    def local(src, dst):
        copy = pltpu.make_async_copy(src, dst, local_sem.at[len(locals_)])
        copy.start()
        locals_.append(copy)
        return copy

    mine = pl.ds(place(0, 0), rows)
    own = [local(tok_in, act.at[0, mine]), local(cot_in, act.at[1, mine])]
    weights = [
        local(gw_in, wgu.at[pl.ds(0, units)]), local(uw_in, wgu.at[pl.ds(units, units)]), local(dw_in, dw)
    ]

    barrier = pltpu.get_barrier_semaphore()
    peers = [sibling, far, near] + [along_x(d) for d in (1, 2, 3)] + [along_z(d) for d in range(1, 8)]
    for peer in peers:
        pl.semaphore_signal(barrier, inc=1, device_id=peer, device_id_type=pl.DeviceIdType.MESH)
    pl.semaphore_wait(barrier, len(peers))

    got, sib = {}, {}

    def rows_at(d, half, other, which=None):
        span = pl.ds(place(d, half) + other * rows, rows)
        return act.at[:, span] if which is None else act.at[which, span]

    def ring(j, half):
        for sign in (1, -1):
            which = None if j < 4 else (0 if sign == 1 else 1)
            src, dst = -sign * (j - 1), (-sign * j if j < 4 else 4)
            got[sign, j, half] = send(
                rows_at(src, half, 0, which), rows_at(dst, half, 0, which), along_z(sign)
            )
            sent_act.append(got[sign, j, half])

    def to_sibling(d, half, which=None):
        sent_act.append(send(rows_at(d, half, 0, which), rows_at(d, half, 1, which), sibling))
        return sent_act[-1]

    waited = []

    def arrive(copy):
        if not any(copy is other for other in waited):
            waited.append(copy)
            copy.wait_recv()

    def a0():
        for copy in own:
            copy.wait()
        sib["far"] = send(rows_at(0, 0, 0), rows_at(0, 1, 0), far)
        sent_act.append(sib["far"])
        ring(1, 0)
        sib[0, 0] = [to_sibling(0, 0)]
        for copy in weights:
            copy.wait()
        wt[...] = wgu[...].T
        dt[...] = dw[...].T

    def a1():
        arrive(sib["far"])
        ring(1, 1)
        sib[0, 1] = [to_sibling(0, 1)]

    def forward(j, half):
        for sign in (1, -1):
            arrive(got[sign, j, half])
        if j < 4:
            ring(j + 1, half)
            for d in (j, -j):
                sib[d, half] = [to_sibling(d, half)]
        else:
            sib[4, half] = [to_sibling(4, half, 0), to_sibling(4, half, 1)]

    def ready(k):
        lo, hi = OFFSETS[k], OFFSETS[k] + CHUNKS[k]
        for i, unit in enumerate(UNITS):
            if i * 2 * rows < hi and (i + 1) * 2 * rows > lo:
                for copy in sib[unit]:
                    arrive(copy)

    def sizes(k):
        return OFFSETS[k], CHUNKS[k], CHUNKS[k] // 2, CHUNKS[k] // 8

    def start_sum(a, k, x_first, term):
        o, n, q, r = sizes(k)
        a.own[pl.ds(o, n)] = term
        if x_first:
            a.s1x[:, pl.ds(SAME[k] // 2, q)] = term.astype(BF16).reshape(2, q, -1)
            a.first[k] = [
                send(
                    a.s1x.at[:, at(SAME[k] // 2 + x_of(d) * r, r)],
                    a.r1x.at[d - 1, :, pl.ds(SAME[k] // 8, r)],
                    along_x(d),
                )
                for d in (1, 3, 2)
            ]
        else:
            half = pl.ds(SAME[k] // 2, q)
            a.s1y[half] = a.own[at(o + (1 - yl) * q, q)].astype(BF16)
            a.first[k] = [send(a.s1y.at[half], a.r1y.at[half], near)]

    def go_on(a, k, x_first):
        o, n, q, r = sizes(k)
        half, piece = pl.ds(SAME[k] // 2, q), pl.ds(SAME[k] // 8, r)
        for copy in a.first[k]:
            arrive(copy)
        if x_first:
            def total(y):
                value = a.own[at(o + y * q + x * r, r)]
                for d in range(3):
                    value = value + a.r1x[d, y, piece].astype(F32)
                return value

            a.s2y[piece] = total(1 - yl).astype(BF16)
            a.second[k] = [send(a.s2y.at[piece], a.r2y.at[piece], near)]
            a.fin[piece] = total(yl)
        else:
            a.s2x[half] = (a.own[at(o + yl * q, q)] + a.r1y[half].astype(F32)).astype(BF16)
            a.second[k] = [
                send(a.s2x.at[at(SAME[k] // 2 + x_of(d) * r, r)], a.r2x.at[d - 1, piece], along_x(d))
                for d in (1, 3, 2)
            ]

    def end_sum(a, k, x_first):
        o, n, q, r = sizes(k)
        piece = pl.ds(SAME[k] // 8, r)
        for copy in a.second[k]:
            arrive(copy)
        if x_first:
            return a.fin[piece] + a.r2y[piece].astype(F32)
        value = a.own[at(o + yl * q + x * r, r)] + a.r1y[at(SAME[k] // 2 + x * r, r)].astype(F32)
        for d in range(3):
            value = value + a.r2x[d, piece].astype(F32)
        return value

    def s1a(k):
        ready(k)
        start_sum(gu, k, X_FIRST[k], dot(act[0, pl.ds(OFFSETS[k], CHUNKS[k])], wt[...], 1, 0))

    def s1b(k):
        ready(k)
        start_sum(h, k, not X_FIRST[k], dot(act[1, pl.ds(OFFSETS[k], CHUNKS[k])], dt[...], 1, 0))

    def s2a(k):
        go_on(h if X_FIRST[k] else gu, k, False)

    def s2b(k):
        go_on(gu if X_FIRST[k] else h, k, True)

    pa_y, pa_x, pb_y, pb_x, pa_xx, pb_yy = {}, {}, {}, {}, {}, {}

    def rows_of(k, y, of):
        o, n, q, r = sizes(k)
        return at(o + y * q + of * r, r)

    def same(ref, span, device):
        return send(ref.at[span], ref.at[span], device)

    def ways(k):
        return (1, 3) if FORWARD[k] else (1, 3, 2)

    def s3(k):
        g = end_sum(gu, k, X_FIRST[k])
        hidden_grad = end_sum(h, k, not X_FIRST[k])
        gate, up = g[:, :units], g[:, units:]
        sigmoid_gate = jax.nn.sigmoid(gate)
        span = rows_of(k, yl, x)
        up_part = hidden_grad * gate * sigmoid_gate
        gate_part = hidden_grad * up * sigmoid_gate * (1.0 + gate * (1.0 - sigmoid_gate))
        pa[span] = jnp.concatenate([gate_part, up_part], axis=1).astype(BF16)
        pa_y[k] = same(pa, span, near)
        pa_x[k] = {d: same(pa, span, along_x(d)) for d in ways(k)}
        pb[span] = (gate * sigmoid_gate * up).astype(BF16)

    def s3b(k):
        span = rows_of(k, yl, x)
        pb_x[k] = {d: same(pb, span, along_x(d)) for d in ways(k)}
        pb_y[k] = same(pb, span, near)

    def s4a(k):
        arrive(pa_y[k])
        span = rows_of(k, 1 - yl, x)
        pa_xx[k] = {d: same(pa, span, along_x(d)) for d in ways(k)}

    def s4f1(k):
        arrive(pa_x[k][1])
        pa_x[k][2] = same(pa, rows_of(k, yl, x_of(3)), along_x(1))

    def s4f2(k):
        arrive(pa_xx[k][3])
        pa_xx[k][2] = same(pa, rows_of(k, 1 - yl, x_of(1)), along_x(3))

    def s4b(k):
        pb_yy[k] = []
        for d in ways(k):
            arrive(pb_x[k][d])
            pb_yy[k].append(same(pb, rows_of(k, yl, x_of(4 - d)), near))
        if FORWARD[k]:
            d = 1 if k % 2 else 3
            pb_x[k][2] = same(pb, rows_of(k, yl, x_of(4 - d)), along_x(d))

    def s4c(k):
        arrive(pb_x[k][2])
        pb_yy[k].append(same(pb, rows_of(k, yl, x_of(2)), near))

    def s5(k):
        for copy in (*pa_x[k].values(), *pa_xx[k].values()):
            arrive(copy)
        span = pl.ds(OFFSETS[k], CHUNKS[k])
        ip[span] = dot(pa[span], wgu[...], 1, 0)

    summed = []

    def s6(g):
        for k in GROUPS[g]:
            for copy in [pb_y[k]] + pb_yy[k]:
                arrive(copy)
        span = pl.ds(OFFSETS[GROUPS[g][0]], sum(CHUNKS[k] for k in GROUPS[g]))
        gu_term = dot(pa[span], act[0, span], 0, 0)
        acc_gu[...] = acc_gu[...] + gu_term if summed else gu_term
        d_term = dot(pb[span], act[1, span], 0, 0)
        acc_d[...] = acc_d[...] + d_term if summed else d_term
        summed.append(g)

    dc, dy, dz = {}, {}, {}

    def d1(s, half):
        start = place(SLOTS[s], half)
        dc[s, half] = send(ip.at[pl.ds(start + rows, rows)], d_r1.at[s, half], sibling)

    def both(s, half):
        arrive(dc[s, half])
        return ip[pl.ds(place(SLOTS[s], half), rows)] + d_r1[s, half]

    def d2(s):
        value = both(s, 1)
        if s == 0:
            for i, d in enumerate(NEAR_Z):
                arrive(dz[SLOTS.index(d)])
                value = value + d_rz[i, 1].astype(F32)
        d_s2[s] = value.astype(BF16)
        dy[s] = send(d_s2.at[s], d_r2.at[s], far)

    def d3(s):
        if SLOTS[s] in NEAR_Z:
            i = NEAR_Z.index(SLOTS[s])
            for half in (0, 1):
                d_sz[i, half] = both(s, half).astype(BF16)
            dz[s] = send(d_sz.at[i], d_rz.at[i], along_z(SLOTS[s]))
        else:
            value = both(s, 0)
            arrive(dy[s])
            d_s3[s] = (value + d_r2[s].astype(F32)).astype(BF16)
            dz[s] = send(d_s3.at[s], d_r3.at[s - 1], along_z(SLOTS[s]))

    outs = []

    def d4():
        value = both(0, 0)
        arrive(dy[0])
        value = value + d_r2[0].astype(F32)
        for s in range(1, 8):
            arrive(dz[s])
            if SLOTS[s] in NEAR_Z:
                value = value + d_rz[NEAR_Z.index(SLOTS[s]), 0].astype(F32)
            else:
                value = value + d_r3[s - 1].astype(F32)
        ig_v[...] = value.astype(BF16)
        outs.append(local(ig_v, ig_out))

    def fin():
        for copy in sent_act:
            copy.wait_send()
        first, second = pl.ds(0, units), pl.ds(units, units)
        act[0, pl.ds(0, 2 * units)] = acc_gu[...].astype(BF16)
        outs.append(local(act.at[0, first], gg_out))
        outs.append(local(act.at[0, second], ug_out))
        act[1, first] = acc_d[...].astype(BF16)
        outs.append(local(act.at[1, first], dg_out))

    steps = {
        "A0": a0, "A1": a1, "R": forward, "s1a": s1a, "s1b": s1b, "s2a": s2a, "s2b": s2b, "s3": s3, "s3b": s3b,
        "s4a": s4a, "s4f1": s4f1, "s4f2": s4f2, "s4b": s4b, "s4c": s4c, "s5": s5, "s6": s6,
        "d1": d1, "d2": d2, "d3": d3, "d4": d4, "fin": fin,
    }
    for name, *where in ORDER:
        steps[name](*where)
    for copy in copies:
        if not any(copy is other for other in sent_act):
            copy.wait_send()
    for copy in outs:
        copy.wait()


def hand_over(*refs):
    n = len(refs) // 2
    for i in range(n):
        refs[n + i][...] = refs[i][...]


def on_device(tokens, cotangent, gate_weight, up_weight, down_weight):
    rows, width = tokens.shape
    units = down_weight.shape[0]
    n = rows * 32
    scratch = [
        ((2, n, width), BF16), ((2 * units, width), BF16), ((units, width), BF16),
        *Sum.shapes(2 * units, X_ROWS, Y_ROWS), *Sum.shapes(units, Y_ROWS, X_ROWS),
        ((n, 2 * units), BF16), ((n, units), BF16), ((n, width), F32),
        ((8, 2, rows, width), F32), ((8, rows, width), BF16), ((8, rows, width), BF16),
        ((8, rows, width), BF16), ((7, rows, width), BF16),
        ((max(len(NEAR_Z), 1), 2, rows, width), BF16), ((max(len(NEAR_Z), 1), 2, rows, width), BF16),
        ((2 * units, width), F32), ((units, width), F32),
        ((rows, width), BF16), ((width, 2 * units), BF16), ((width, units), BF16),
    ]
    results = [
        jax.ShapeDtypeStruct(a.shape, BF16) for a in (tokens, down_weight, down_weight, down_weight)
    ]
    values = pl.pallas_call(
        kernel,
        out_shape=results,
        in_specs=[pl.BlockSpec(memory_space=pl.ANY)] * 5,
        out_specs=[pl.BlockSpec(memory_space=pl.ANY)] * 4,
        scratch_shapes=[pltpu.VMEM(shape, dtype) for shape, dtype in scratch]
        + [
            pltpu.SemaphoreType.DMA((COPIES,)),
            pltpu.SemaphoreType.DMA((COPIES,)),
            pltpu.SemaphoreType.DMA((16,)),
        ],
        compiler_params=pltpu.CompilerParams(
            collective_id=0, has_side_effects=True, vmem_limit_bytes=61 * 2**20
        ),
        cost_estimate=pl.CostEstimate(
            flops=16 * n * width * units, bytes_accessed=6 * 2**20, transcendentals=n * units // 8
        ),
    )(tokens, cotangent, gate_weight.T, up_weight.T, down_weight)
    input_grad, gate_grad, up_grad, down_grad = pl.pallas_call(
        hand_over,
        out_shape=results,
    )(*values)
    return input_grad, gate_grad.T, up_grad.T, down_grad


def solution(mesh):
    blocks = ("gx", "gy")
    by_row, by_column = P(blocks, "gz"), P("gz", blocks)
    return jax.shard_map(
        on_device,
        mesh=mesh,
        in_specs=(by_row, by_row, by_column, by_column, by_row),
        out_specs=(by_row, by_column, by_column, by_row),
        check_vma=False,
    )
```
